32 devices in a mesh: sec: 4 (over z), col: 4 (over y, x), sect: 2 (over core).
Axes of the slice: x: 2, y: 2, z: 4, core: 2. Of those that a mesh axis runs over, the one named last changes fastest.
Arguments:
- transfer: float32 [16, 16, 2, 256, 256], P('sec', ('col', 'sect')), may hold values from -1 to 2
- trunc_ranks: int32 [16, 16, 2], P('sec', ('col', 'sect')), may hold values from 64 to 256
Outputs:
- gradient: float32 [16, 16, 2, 256, 256], P('sec', 'col', 'sect')
The draws below stay inside these ranges and needn't reach their ends.
All inputs are finite; a program needn't handle non-finite values.
Results may differ from the reference program's by a relative error of at most 0.038.
Values sent between devices are 32-bit elements; how exact they have to be, the bound alone decides.
A program may use at most 192 MiB of HBM per device.

```python
import math
import jax
import jax.numpy as jnp
from jax import lax

H = 256
ALL_ROWS = 16
ALL_COLS = 16


def draw_transfer(key, part):
    shape = (ALL_ROWS, ALL_COLS, 2, H, H)
    noise = jax.random.normal(key, shape, jnp.float32)
    coupling = jnp.full((H, H), 0.5 / H, dtype=jnp.float32)
    return jnp.eye(H, dtype=jnp.float32) + coupling + 0.08 / math.sqrt(H) * noise


def touch_ends(array, own_key, low, largest):
    dims = array.shape
    place = [jax.random.randint(jax.random.fold_in(own_key, axis), (), 0, dims[axis]) for axis in range(len(dims))]
    array = array.at[tuple(place)].set(low)
    longest = dims.index(max(dims))
    place[longest] = (place[longest] + 1) % dims[longest]
    return array.at[tuple(place)].set(largest)


def setup_inputs(seed: int = 0) -> dict:
    key_list = jax.random.split(jax.random.key(seed), 3)
    return {
        "transfer": draw_transfer(jax.random.fold_in(key_list[2], 71), 0),
        "trunc_ranks": touch_ends(jax.random.randint(key_list[1], (ALL_ROWS, ALL_COLS, 2), H // 4, H + 1), jax.random.fold_in(key_list[1], 1), H // 4, H).astype(jnp.int32),
    }


def product(former, latter):
    return jnp.einsum('...ik,...kj->...ij', former, latter, precision=lax.Precision.HIGHEST)

def flipped(matrix):
    return jnp.swapaxes(matrix, -1, -2)

def orthonormal(row_envs, trunc_ranks):
    bond_width = row_envs.shape[-1]
    unit_matrix = jnp.eye(bond_width, dtype=jnp.float32)
    kept_mask = (jnp.arange(bond_width, dtype=jnp.int32) < trunc_ranks[..., None]).astype(jnp.float32)
    truncated = kept_mask[..., :, None] * row_envs * kept_mask[..., None, :] + unit_matrix * (1.0 - kept_mask)[..., None, :]
    gram_matrix = product(flipped(truncated), truncated)
    lower_factor = jnp.linalg.cholesky(gram_matrix)
    solved = lax.linalg.triangular_solve(lower_factor, flipped(truncated), left_side=True, lower=True)
    return flipped(solved)

def reference(transfer, trunc_ranks):
    unit_block = jnp.broadcast_to(jnp.eye(H, dtype=jnp.float32), transfer.shape[1:])

    def absorb_down(running, factor):
        return (product(factor, running), running)
    _, env_above = lax.scan(absorb_down, unit_block, transfer)

    def absorb_up(running, inputs):
        factor, upper = inputs
        return (product(running, factor), flipped(product(upper, running)))
    _, row_envs = lax.scan(absorb_up, unit_block, (transfer, env_above), reverse=True)
    blocks = lax.map(lambda pair: orthonormal(pair[0], pair[1]), (row_envs, trunc_ranks))
    by_column = jnp.moveaxis(blocks, 1, 0)
    column_unit = jnp.broadcast_to(jnp.eye(H, dtype=jnp.float32), by_column.shape[1:])

    def sweep_left(running, factor):
        return (product(running, factor), running)

    def sweep_right(running, factor):
        return (product(factor, running), running)
    _, left_envs = lax.scan(sweep_left, column_unit, by_column)
    _, right_envs = lax.scan(sweep_right, column_unit, by_column, reverse=True)
    gradient = math.sqrt(H) * flipped(product(right_envs, left_envs))
    return jnp.moveaxis(gradient, 0, 1)
```

```python
import functools
import math

import jax
import jax.numpy as jnp
from jax import lax
from jax.experimental import pallas as pl
from jax.experimental.pallas import tpu as pltpu
from jax.sharding import PartitionSpec as P

PANEL = 32
PACK = 128 // PANEL


def product(former, latter):
    return jnp.einsum("...ik,...kj->...ij", former, latter, precision=lax.Precision.HIGHEST)


def split3(value):
    first = value.astype(jnp.bfloat16)
    rest = value - first.astype(jnp.float32)
    second = rest.astype(jnp.bfloat16)
    third = (rest - second.astype(jnp.float32)).astype(jnp.bfloat16)
    return first, second, third


def stack_left(value, axis):
    a, b, c = split3(value)
    return jnp.concatenate([a, a, b, a, b, c], axis=axis)


def stack_right(value, axis):
    a, b, c = split3(value)
    return jnp.concatenate([a, b, a, c, b, a], axis=axis)


def panel_inverse(groups):
    lane = lax.broadcasted_iota(jnp.int32, (8, 128), 1)
    sub = lax.broadcasted_iota(jnp.int32, (8, 128), 0)
    local = lane % PANEL
    base = lane - local
    tiles = PANEL // 8
    work = [[g[8 * r : 8 * r + 8] for r in range(tiles)] for g in groups]
    inv = [
        [jnp.where(local == sub + 8 * r, 1.0, 0.0).astype(jnp.float32) for r in range(tiles)]
        for _ in groups
    ]
    for k in range(PANEL):
        own, at = divmod(k, 8)
        index = base + k
        for a, w in zip(work, inv):
            cols = [
                jnp.take_along_axis(a[r], index, axis=1, mode="promise_in_bounds")
                for r in range(own, tiles)
            ]
            pivot = cols[0][at : at + 1]
            recip = 1.0 / pivot
            row_a = a[own][at : at + 1] * recip
            row_w = w[own][at : at + 1] * recip
            scale = lax.rsqrt(pivot)
            for r in range(own, tiles):
                m = cols[r - own]
                if r == own:
                    m = jnp.where(sub > at, m, 0.0)
                a[r] = a[r] - m * row_a
                w[r] = w[r] - m * row_w
            w[own] = w[own] * jnp.where(sub == at, scale, 1.0)
    return [jnp.concatenate(w, axis=0) for w in inv]


def orthonormal_kernel(rank_ref, env_ref, out_ref, gram_ref, inv_ref):
    count, width, _ = env_ref.shape

    def start(m, carry):
        rank = rank_ref[m]
        row = lax.broadcasted_iota(jnp.int32, (width, width), 0)
        col = lax.broadcasted_iota(jnp.int32, (width, width), 1)
        kept = jnp.logical_and(row < rank, col < rank)
        unit = jnp.where(jnp.logical_and(row == col, row >= rank), 1.0, 0.0)
        value = jnp.where(kept, env_ref[m], unit)
        out_ref[m] = value
        gram_ref[m] = lax.dot_general(
            value,
            value,
            (((1,), (1,)), ((), ())),
            precision=lax.Precision.HIGHEST,
            preferred_element_type=jnp.float32,
        )
        return carry

    lax.fori_loop(0, count, start, 0)

    for p in range(width // PANEL):
        lo, hi = p * PANEL, (p + 1) * PANEL
        edge = lo // 128 * 128
        groups = [
            jnp.concatenate(
                [gram_ref[g * PACK + i, lo:hi, edge : edge + 128][:, lo - edge : hi - edge] for i in range(PACK)],
                axis=1,
            )
            for g in range(count // PACK)
        ]
        for g, packed in enumerate(panel_inverse(groups)):
            for i in range(PACK):
                inv_ref[g * PACK + i] = packed[:, i * PANEL : (i + 1) * PANEL]

        def update(m, carry):
            factor = stack_left(inv_ref[m], 1)
            rows_g = stack_right(gram_ref[m, lo:hi, edge:], 0)
            rows_r = stack_right(out_ref[m, lo:hi, :], 0)
            upper = jnp.dot(factor, rows_g, preferred_element_type=jnp.float32)
            done = jnp.dot(factor, rows_r, preferred_element_type=jnp.float32)
            out_ref[m, lo:hi, :] = done
            if hi < width:
                low = stack_left(upper, 0)
                low = low[:, (hi // 128 * 128) - edge :]
                skip = hi % 128
                first = hi // 128 * 128
                contract = (((0,), (0,)), ((), ()))
                tail_r = lax.dot_general(
                    low, stack_right(done, 0), contract, preferred_element_type=jnp.float32
                )
                tail_g = lax.dot_general(
                    low,
                    stack_right(upper, 0)[:, first - edge :],
                    contract,
                    preferred_element_type=jnp.float32,
                )
                out_ref[m, hi:, :] = out_ref[m, hi:, :] - tail_r[skip:]
                gram_ref[m, hi:, first:] = gram_ref[m, hi:, first:] - tail_g[skip:]
            return carry

        lax.fori_loop(0, count, update, 0)


def orthonormal(envs, ranks):
    count, width, _ = envs.shape
    vmem = pl.BlockSpec(memory_space=pltpu.VMEM)
    return pl.pallas_call(
        orthonormal_kernel,
        out_shape=jax.ShapeDtypeStruct(envs.shape, jnp.float32),
        in_specs=[pl.BlockSpec(memory_space=pltpu.SMEM), vmem],
        out_specs=vmem,
        scratch_shapes=[
            pltpu.VMEM((count, width, width), jnp.float32),
            pltpu.VMEM((count, PANEL, PANEL), jnp.float32),
        ],
        compiler_params=pltpu.CompilerParams(vmem_limit_bytes=40 * 2**20),
    )(ranks, envs)


def around(parts, axis):
    n = len(parts)
    above = [None, parts[0]]
    for r in range(1, n):
        above.append(product(parts[r], above[-1]))
    below = [None, parts[n - 1]]
    for r in range(n - 2, 0, -1):
        below.append(product(below[-1], parts[r]))
    below = below[::-1]
    total = above[n]
    devices = lax.axis_size(axis)
    me = lax.axis_index(axis)
    gathered = lax.all_gather(total, axis)
    middle = lax.dynamic_index_in_dim(gathered, (me + devices - 1) % devices, 0, False)
    for k in range(2, devices):
        other = lax.dynamic_index_in_dim(gathered, (me + devices - k) % devices, 0, False)
        middle = product(middle, other)
    result = []
    for r in range(n):
        value = middle
        if r:
            value = product(above[r], value)
        if r < n - 1:
            value = product(value, below[r])
        result.append(value)
    return result


def on_device(transfer, trunc_ranks):
    rows, cols, sectors, width, _ = transfer.shape
    envs = jnp.stack(around([transfer[r] for r in range(rows)], "sec"))
    blocks = orthonormal(envs.reshape(-1, width, width), trunc_ranks.reshape(-1))
    blocks = blocks.reshape(transfer.shape)
    owned = lax.all_to_all(blocks, "sect", split_axis=2, concat_axis=1, tiled=True)
    result = around([owned[:, c] for c in range(owned.shape[1])], "col")
    return math.sqrt(width) * jnp.stack(result, axis=1)


def solution(mesh):
    in_specs = (P("sec", ("col", "sect"), None, None, None), P("sec", ("col", "sect"), None))
    out_specs = P("sec", "col", "sect", None, None)
    return jax.shard_map(
        on_device, mesh=mesh, in_specs=in_specs, out_specs=out_specs, check_vma=False
    )
```

```python
import functools
import math

import jax
import jax.numpy as jnp
from jax import lax
from jax.experimental import pallas as pl
from jax.experimental.pallas import tpu as pltpu
from jax.sharding import PartitionSpec as P

PANEL = 32
PACK = 128 // PANEL


def product(former, latter, precision=lax.Precision.HIGHEST):
    return jnp.einsum("...ik,...kj->...ij", former, latter, precision=precision)


def split3(value):
    first = value.astype(jnp.bfloat16)
    rest = value - first.astype(jnp.float32)
    second = rest.astype(jnp.bfloat16)
    third = (rest - second.astype(jnp.float32)).astype(jnp.bfloat16)
    return first, second, third


def stack_left(value, axis):
    a, b, c = split3(value)
    return jnp.concatenate([a, a, b, a, b, c], axis=axis)


def stack_right(value, axis):
    a, b, c = split3(value)
    return jnp.concatenate([a, b, a, c, b, a], axis=axis)


def panel_inverse(groups):
    lane = lax.broadcasted_iota(jnp.int32, (8, 128), 1)
    sub = lax.broadcasted_iota(jnp.int32, (8, 128), 0)
    local = lane % PANEL
    base = lane - local
    tiles = PANEL // 8
    work = [[g[8 * r : 8 * r + 8] for r in range(tiles)] for g in groups]
    inv = [
        [jnp.where(local == sub + 8 * r, 1.0, 0.0).astype(jnp.float32) for r in range(tiles)]
        for _ in groups
    ]
    for k in range(PANEL):
        own, at = divmod(k, 8)
        index = base + k
        for a, w in zip(work, inv):
            cols = [
                jnp.take_along_axis(a[r], index, axis=1, mode="promise_in_bounds")
                for r in range(own, tiles)
            ]
            pivot = cols[0][at : at + 1]
            recip = 1.0 / pivot
            row_a = a[own][at : at + 1] * recip
            row_w = w[own][at : at + 1] * recip
            scale = lax.rsqrt(pivot)
            for r in range(own, tiles):
                m = cols[r - own]
                if r == own:
                    m = jnp.where(sub > at, m, 0.0)
                a[r] = a[r] - m * row_a
                w[r] = w[r] - m * row_w
            w[own] = w[own] * jnp.where(sub == at, scale, 1.0)
    return [jnp.concatenate(w, axis=0) for w in inv]


def orthonormal_kernel(rank_ref, env_ref, out_ref, gram_ref, inv_ref):
    count, width, _ = env_ref.shape

    def start(m, carry):
        rank = rank_ref[m]
        row = lax.broadcasted_iota(jnp.int32, (width, width), 0)
        col = lax.broadcasted_iota(jnp.int32, (width, width), 1)
        kept = jnp.logical_and(row < rank, col < rank)
        unit = jnp.where(jnp.logical_and(row == col, row >= rank), 1.0, 0.0)
        value = jnp.where(kept, env_ref[m], unit)
        out_ref[m] = value
        gram_ref[m] = lax.dot_general(
            value,
            value,
            (((1,), (1,)), ((), ())),
            precision=lax.Precision.HIGHEST,
            preferred_element_type=jnp.float32,
        )
        return carry

    lax.fori_loop(0, count, start, 0)

    for p in range(width // PANEL):
        lo, hi = p * PANEL, (p + 1) * PANEL
        edge = lo // 128 * 128
        groups = [
            jnp.concatenate(
                [gram_ref[g * PACK + i, lo:hi, edge : edge + 128][:, lo - edge : hi - edge] for i in range(PACK)],
                axis=1,
            )
            for g in range(count // PACK)
        ]
        for g, packed in enumerate(panel_inverse(groups)):
            for i in range(PACK):
                inv_ref[g * PACK + i] = packed[:, i * PANEL : (i + 1) * PANEL]

        def update(m, carry):
            factor = stack_left(inv_ref[m], 1)
            rows_g = stack_right(gram_ref[m, lo:hi, edge:], 0)
            rows_r = stack_right(out_ref[m, lo:hi, :], 0)
            upper = jnp.dot(factor, rows_g, preferred_element_type=jnp.float32)
            done = jnp.dot(factor, rows_r, preferred_element_type=jnp.float32)
            out_ref[m, lo:hi, :] = done
            if hi < width:
                low = stack_left(upper, 0)
                low = low[:, (hi // 128 * 128) - edge :]
                skip = hi % 128
                first = hi // 128 * 128
                contract = (((0,), (0,)), ((), ()))
                tail_r = lax.dot_general(
                    low, stack_right(done, 0), contract, preferred_element_type=jnp.float32
                )
                tail_g = lax.dot_general(
                    low,
                    stack_right(upper, 0)[:, first - edge :],
                    contract,
                    preferred_element_type=jnp.float32,
                )
                out_ref[m, hi:, :] = out_ref[m, hi:, :] - tail_r[skip:]
                gram_ref[m, hi:, first:] = gram_ref[m, hi:, first:] - tail_g[skip:]
            return carry

        lax.fori_loop(0, count, update, 0)


def orthonormal(envs, ranks):
    count, width, _ = envs.shape
    vmem = pl.BlockSpec(memory_space=pltpu.VMEM)
    return pl.pallas_call(
        orthonormal_kernel,
        out_shape=jax.ShapeDtypeStruct(envs.shape, jnp.float32),
        in_specs=[pl.BlockSpec(memory_space=pltpu.SMEM), vmem],
        out_specs=vmem,
        scratch_shapes=[
            pltpu.VMEM((count, width, width), jnp.float32),
            pltpu.VMEM((count, PANEL, PANEL), jnp.float32),
        ],
        compiler_params=pltpu.CompilerParams(vmem_limit_bytes=40 * 2**20),
    )(ranks, envs)


def chain_kernel(axis, n, tot_ref, out_ref, up, down, up_out, down_out, send_u, recv_u, send_d, recv_d):
    count, width, _ = tot_ref.shape
    half = width // 2
    me = lax.axis_index(axis)
    has_prev, has_next = me > 0, me < n - 1
    inner = jnp.logical_and(has_prev, has_next)

    def up_copy(q):
        return pltpu.make_async_remote_copy(
            src_ref=up_out.at[q],
            dst_ref=up.at[q],
            send_sem=send_u.at[q],
            recv_sem=recv_u.at[q],
            device_id={axis: jnp.minimum(me + 1, n - 1)},
            device_id_type=pl.DeviceIdType.MESH,
        )

    def down_copy(q):
        return pltpu.make_async_remote_copy(
            src_ref=down_out.at[q],
            dst_ref=down.at[q],
            send_sem=send_d.at[q],
            recv_sem=recv_d.at[q],
            device_id={axis: jnp.maximum(me - 1, 0)},
            device_id_type=pl.DeviceIdType.MESH,
        )

    def dot(a, b):
        return jnp.dot(
            a, b, precision=lax.Precision.HIGHEST, preferred_element_type=jnp.float32
        )

    barrier = pltpu.get_barrier_semaphore()

    @pl.when(has_prev)
    def _():
        pl.semaphore_signal(
            barrier, inc=1, device_id={axis: me - 1}, device_id_type=pl.DeviceIdType.MESH
        )

    @pl.when(has_next)
    def _():
        pl.semaphore_signal(
            barrier, inc=1, device_id={axis: me + 1}, device_id_type=pl.DeviceIdType.MESH
        )

    @pl.when(inner)
    def _():
        pl.semaphore_wait(barrier, 2)

    @pl.when(jnp.logical_not(inner))
    def _():
        pl.semaphore_wait(barrier, 1)

    @pl.when(me == 0)
    def _():
        def send(c, carry):
            for h in range(2):
                up_out[2 * c + h] = tot_ref[c, :, h * half : (h + 1) * half]
                up_copy(2 * c + h).start()
            return carry

        lax.fori_loop(0, count, send, 0)

    @pl.when(me == n - 1)
    def _():
        def send(c, carry):
            for h in range(2):
                down_out[2 * c + h] = tot_ref[c, h * half : (h + 1) * half, :]
                down_copy(2 * c + h).start()
            return carry

        lax.fori_loop(0, count, send, 0)

    def one(c, carry):
        for h in range(2):
            q = 2 * c + h

            @pl.when(has_prev)
            def _():
                up_copy(q).wait_recv()

            @pl.when(inner)
            def _():
                up_out[q] = dot(tot_ref[c], up[q])
                up_copy(q).start()

            @pl.when(has_next)
            def _():
                down_copy(q).wait_recv()

            @pl.when(inner)
            def _():
                down_out[q] = dot(down[q], tot_ref[c])
                down_copy(q).start()

        @pl.when(inner)
        def _():
            out_ref[c] = dot(up[2 * c], down[2 * c]) + dot(up[2 * c + 1], down[2 * c + 1])

        @pl.when(me == 0)
        def _():
            for h in range(2):
                out_ref[c, h * half : (h + 1) * half, :] = down[2 * c + h]

        @pl.when(me == n - 1)
        def _():
            for h in range(2):
                out_ref[c, :, h * half : (h + 1) * half] = up[2 * c + h]

        return carry

    lax.fori_loop(0, count, one, 0)

    def drain(q, carry):
        @pl.when(has_next)
        def _():
            up_copy(q).wait_send()

        @pl.when(has_prev)
        def _():
            down_copy(q).wait_send()

        return carry

    lax.fori_loop(0, 2 * count, drain, 0)


def chain_middle(total, axis):
    shape = total.shape
    width = shape[-1]
    total = total.reshape(-1, width, width)
    count = total.shape[0]
    vmem = pl.BlockSpec(memory_space=pltpu.VMEM)
    tall = pltpu.VMEM((2 * count, width, width // 2), jnp.float32)
    wide = pltpu.VMEM((2 * count, width // 2, width), jnp.float32)
    middle = pl.pallas_call(
        functools.partial(chain_kernel, axis, lax.axis_size(axis)),
        out_shape=jax.ShapeDtypeStruct(total.shape, jnp.float32),
        in_specs=[vmem],
        out_specs=vmem,
        scratch_shapes=[tall, wide, tall, wide] + [pltpu.SemaphoreType.DMA((2 * count,))] * 4,
        compiler_params=pltpu.CompilerParams(
            collective_id=0, has_side_effects=True, vmem_limit_bytes=32 * 2**20
        ),
    )(total)
    return middle.reshape(shape)


def pair_middle(total, axis, precision):
    odd = lax.axis_index(axis) % 2 == 1
    result = []
    for i in range(total.shape[0]):
        own = total[i]
        other = lax.ppermute(own, axis, [(0, 1), (1, 0), (2, 3), (3, 2)])
        pair = product(jnp.where(odd, own, other), jnp.where(odd, other, own), precision)
        far = lax.ppermute(pair, axis, [(0, 2), (2, 0), (1, 3), (3, 1)])
        result.append(product(jnp.where(odd, other, far), jnp.where(odd, far, other), precision))
    return jnp.stack(result)


def gathered_middle(total, axis, precision):
    devices = lax.axis_size(axis)
    me = lax.axis_index(axis)
    gathered = lax.all_gather(total, axis)
    middle = lax.dynamic_index_in_dim(gathered, (me + devices - 1) % devices, 0, False)
    for k in range(2, devices):
        other = lax.dynamic_index_in_dim(gathered, (me + devices - k) % devices, 0, False)
        middle = product(middle, other, precision)
    return middle


def around(parts, middle_of, precision):
    n = len(parts)
    above = [None, parts[0]]
    below = [None, parts[n - 1]]
    for r in range(1, n):
        above.append(product(parts[r], above[-1], precision))
    for r in range(n - 2, 0, -1):
        below.append(product(below[-1], parts[r], precision))
    below = below[::-1]
    middle = middle_of(above[n])
    result = []
    for r in range(n):
        value = middle
        if r:
            value = product(above[r], value, precision)
        if r < n - 1:
            value = product(value, below[r], precision)
        result.append(value)
    return result


def on_device(transfer, trunc_ranks):
    rows, cols, sectors, width, _ = transfer.shape
    exact, fine = lax.Precision.HIGHEST, lax.Precision.HIGH
    parts = [transfer[r] for r in range(rows)]
    envs = jnp.stack(around(parts, lambda t: chain_middle(t, "sec"), exact))
    blocks = orthonormal(envs.reshape(-1, width, width), trunc_ranks.reshape(-1))
    blocks = blocks.reshape(transfer.shape)
    owned = lax.all_to_all(blocks, "sect", split_axis=2, concat_axis=1, tiled=True)
    columns = [owned[:, c] for c in range(owned.shape[1])]
    middle_of = pair_middle if lax.axis_size("col") == 4 else gathered_middle
    result = around(columns, lambda t: middle_of(t, "col", fine), fine)
    return math.sqrt(width) * jnp.stack(result, axis=1)


def solution(mesh):
    in_specs = (P("sec", ("col", "sect"), None, None, None), P("sec", ("col", "sect"), None))
    out_specs = P("sec", "col", "sect", None, None)
    return jax.shard_map(
        on_device, mesh=mesh, in_specs=in_specs, out_specs=out_specs, check_vma=False
    )
```

```python
import functools
import math

import jax
import jax.numpy as jnp
from jax import lax
from jax.experimental import pallas as pl
from jax.experimental.pallas import tpu as pltpu
from jax.sharding import PartitionSpec as P

PANEL = 32
PACK = 128 // PANEL
LAG = 3
TOGETHER = 4


def product(former, latter, precision=lax.Precision.HIGHEST):
    return jnp.einsum("...ik,...kj->...ij", former, latter, precision=precision)


def split3(value):
    first = value.astype(jnp.bfloat16)
    rest = value - first.astype(jnp.float32)
    second = rest.astype(jnp.bfloat16)
    third = (rest - second.astype(jnp.float32)).astype(jnp.bfloat16)
    return first, second, third


def stack_left(value, axis):
    a, b, c = split3(value)
    return jnp.concatenate([a, a, b, a, b, c], axis=axis)


def stack_right(value, axis):
    a, b, c = split3(value)
    return jnp.concatenate([a, b, a, c, b, a], axis=axis)


def panel_inverse(groups):
    lane = lax.broadcasted_iota(jnp.int32, (8, 128), 1)
    sub = lax.broadcasted_iota(jnp.int32, (8, 128), 0)
    local = lane % PANEL
    base = lane - local
    tiles = PANEL // 8
    work = [[g[8 * r : 8 * r + 8] for r in range(tiles)] for g in groups]
    inv = [
        [jnp.where(local == sub + 8 * r, 1.0, 0.0).astype(jnp.float32) for r in range(tiles)]
        for _ in groups
    ]
    for k in range(PANEL):
        own, at = divmod(k, 8)
        index = base + k
        for a, w in zip(work, inv):
            cols = [
                jnp.take_along_axis(a[r], index, axis=1, mode="promise_in_bounds")
                for r in range(own, tiles)
            ]
            pivot = cols[0][at : at + 1]
            recip = 1.0 / pivot
            row_a = a[own][at : at + 1] * recip
            row_w = w[own][at : at + 1] * recip
            scale = lax.rsqrt(pivot)
            for r in range(own, tiles):
                m = cols[r - own]
                if r == own:
                    m = jnp.where(sub > at, m, 0.0)
                a[r] = a[r] - m * row_a
                w[r] = w[r] - m * row_w
            w[own] = w[own] * jnp.where(sub == at, scale, 1.0)
    return [jnp.concatenate(w, axis=0) for w in inv]


def orthonormal_kernel(rank_ref, env_ref, out_ref, gram_ref, inv_ref):
    count, width, _ = env_ref.shape

    def start(m, carry):
        rank = rank_ref[m]
        row = lax.broadcasted_iota(jnp.int32, (width, width), 0)
        col = lax.broadcasted_iota(jnp.int32, (width, width), 1)
        kept = jnp.logical_and(row < rank, col < rank)
        unit = jnp.where(jnp.logical_and(row == col, row >= rank), 1.0, 0.0)
        value = jnp.where(kept, env_ref[m], unit)
        out_ref[m] = value
        gram_ref[m] = lax.dot_general(
            value,
            value,
            (((1,), (1,)), ((), ())),
            precision=lax.Precision.HIGHEST,
            preferred_element_type=jnp.float32,
        )
        return carry

    lax.fori_loop(0, count, start, 0)

    for p in range(width // PANEL):
        lo, hi = p * PANEL, (p + 1) * PANEL
        edge = lo // 128 * 128
        groups = [
            jnp.concatenate(
                [gram_ref[g * PACK + i, lo:hi, edge : edge + 128][:, lo - edge : hi - edge] for i in range(PACK)],
                axis=1,
            )
            for g in range(count // PACK)
        ]
        for g, packed in enumerate(panel_inverse(groups)):
            for i in range(PACK):
                inv_ref[g * PACK + i] = packed[:, i * PANEL : (i + 1) * PANEL]

        def update(step, carry):
            some = [step * TOGETHER + i for i in range(TOGETHER)]
            factors = [stack_left(inv_ref[m], 1) for m in some]
            rows_g = [stack_right(gram_ref[m, lo:hi, edge:], 0) for m in some]
            rows_r = [stack_right(out_ref[m, lo:hi, :], 0) for m in some]
            done = [
                jnp.dot(f, r, preferred_element_type=jnp.float32)
                for f, r in zip(factors, rows_r)
            ]
            if hi < width:
                skip = hi % 128
                first = hi - skip
                contract = (((0,), (0,)), ((), ()))
                upper = [
                    jnp.dot(f, g, preferred_element_type=jnp.float32)[:, first - edge :]
                    for f, g in zip(factors, rows_g)
                ]
                low = [stack_left(u, 0) for u in upper]
                old_r = [out_ref[m, hi:, :] for m in some]
                old_g = [gram_ref[m, hi:, first:] for m in some]
                tail_r = [
                    lax.dot_general(
                        l, stack_right(d, 0), contract, preferred_element_type=jnp.float32
                    )[skip:]
                    for l, d in zip(low, done)
                ]
                tail_g = [
                    lax.dot_general(
                        l, stack_right(u, 0), contract, preferred_element_type=jnp.float32
                    )[skip:]
                    for l, u in zip(low, upper)
                ]
                for m, old, tail in zip(some, old_r, tail_r):
                    out_ref[m, hi:, :] = old - tail
                for m, old, tail in zip(some, old_g, tail_g):
                    gram_ref[m, hi:, first:] = old - tail
            for m, d in zip(some, done):
                out_ref[m, lo:hi, :] = d
            return carry

        lax.fori_loop(0, count // TOGETHER, update, 0)


def orthonormal(envs, ranks):
    count, width, _ = envs.shape
    vmem = pl.BlockSpec(memory_space=pltpu.VMEM)
    return pl.pallas_call(
        orthonormal_kernel,
        out_shape=jax.ShapeDtypeStruct(envs.shape, jnp.float32),
        in_specs=[pl.BlockSpec(memory_space=pltpu.SMEM), vmem],
        out_specs=vmem,
        scratch_shapes=[
            pltpu.VMEM((count, width, width), jnp.float32),
            pltpu.VMEM((count, PANEL, PANEL), jnp.float32),
        ],
        compiler_params=pltpu.CompilerParams(vmem_limit_bytes=40 * 2**20),
    )(ranks, envs)


def chain_kernel(axis, n, tot_ref, out_ref, up, down, up_out, down_out, send_u, recv_u, send_d, recv_d):
    count, width, _ = tot_ref.shape
    half = width // 2
    me = lax.axis_index(axis)
    has_prev, has_next = me > 0, me < n - 1
    inner = jnp.logical_and(has_prev, has_next)

    def up_copy(q):
        return pltpu.make_async_remote_copy(
            src_ref=up_out.at[q],
            dst_ref=up.at[q],
            send_sem=send_u.at[q],
            recv_sem=recv_u.at[q],
            device_id={axis: jnp.minimum(me + 1, n - 1)},
            device_id_type=pl.DeviceIdType.MESH,
        )

    def down_copy(q):
        return pltpu.make_async_remote_copy(
            src_ref=down_out.at[q],
            dst_ref=down.at[q],
            send_sem=send_d.at[q],
            recv_sem=recv_d.at[q],
            device_id={axis: jnp.maximum(me - 1, 0)},
            device_id_type=pl.DeviceIdType.MESH,
        )

    def dot(a, b):
        return jnp.dot(
            a, b, precision=lax.Precision.HIGHEST, preferred_element_type=jnp.float32
        )

    barrier = pltpu.get_barrier_semaphore()

    @pl.when(has_prev)
    def _():
        pl.semaphore_signal(
            barrier, inc=1, device_id={axis: me - 1}, device_id_type=pl.DeviceIdType.MESH
        )

    @pl.when(has_next)
    def _():
        pl.semaphore_signal(
            barrier, inc=1, device_id={axis: me + 1}, device_id_type=pl.DeviceIdType.MESH
        )

    @pl.when(inner)
    def _():
        pl.semaphore_wait(barrier, 2)

    @pl.when(jnp.logical_not(inner))
    def _():
        pl.semaphore_wait(barrier, 1)

    @pl.when(me == 0)
    def _():
        def send(c, carry):
            for h in range(2):
                up_out[2 * c + h] = tot_ref[c, :, h * half : (h + 1) * half]
                up_copy(2 * c + h).start()
            return carry

        lax.fori_loop(0, count, send, 0)

    @pl.when(me == n - 1)
    def _():
        def send(c, carry):
            for h in range(2):
                down_out[2 * c + h] = tot_ref[c, h * half : (h + 1) * half, :]
                down_copy(2 * c + h).start()
            return carry

        lax.fori_loop(0, count, send, 0)

    chunks = 2 * count
    far = me >= n // 2
    up_lag = jnp.where(far, LAG, 0)
    down_lag = jnp.where(far, 0, LAG)

    def one(step, carry):
        qu = step - up_lag
        qd = step - down_lag
        up_now = jnp.logical_and(qu >= 0, qu < chunks)
        down_now = jnp.logical_and(qd >= 0, qd < chunks)

        @pl.when(jnp.logical_and(has_prev, up_now))
        def _():
            up_copy(qu).wait_recv()

        @pl.when(jnp.logical_and(inner, up_now))
        def _():
            up_out[qu] = dot(tot_ref[qu // 2], up[qu])
            up_copy(qu).start()

        @pl.when(jnp.logical_and(has_next, down_now))
        def _():
            down_copy(qd).wait_recv()

        @pl.when(jnp.logical_and(inner, down_now))
        def _():
            down_out[qd] = dot(down[qd], tot_ref[qd // 2])
            down_copy(qd).start()

        both = jnp.logical_and(step > LAG, (step - LAG) % 2 == 1)
        c = (step - LAG) // 2

        @pl.when(jnp.logical_and(inner, both))
        def _():
            out_ref[c] = dot(up[2 * c], down[2 * c]) + dot(up[2 * c + 1], down[2 * c + 1])

        @pl.when(jnp.logical_and(me == 0, both))
        def _():
            for h in range(2):
                out_ref[c, h * half : (h + 1) * half, :] = down[2 * c + h]

        @pl.when(jnp.logical_and(me == n - 1, both))
        def _():
            for h in range(2):
                out_ref[c, :, h * half : (h + 1) * half] = up[2 * c + h]

        return carry

    lax.fori_loop(0, chunks + LAG, one, 0)

    def drain(q, carry):
        @pl.when(has_next)
        def _():
            up_copy(q).wait_send()

        @pl.when(has_prev)
        def _():
            down_copy(q).wait_send()

        return carry

    lax.fori_loop(0, 2 * count, drain, 0)


def chain_middle(total, axis):
    shape = total.shape
    width = shape[-1]
    total = total.reshape(-1, width, width)
    count = total.shape[0]
    vmem = pl.BlockSpec(memory_space=pltpu.VMEM)
    tall = pltpu.VMEM((2 * count, width, width // 2), jnp.float32)
    wide = pltpu.VMEM((2 * count, width // 2, width), jnp.float32)
    middle = pl.pallas_call(
        functools.partial(chain_kernel, axis, lax.axis_size(axis)),
        out_shape=jax.ShapeDtypeStruct(total.shape, jnp.float32),
        in_specs=[vmem],
        out_specs=vmem,
        scratch_shapes=[tall, wide, tall, wide] + [pltpu.SemaphoreType.DMA((2 * count,))] * 4,
        compiler_params=pltpu.CompilerParams(
            collective_id=0, has_side_effects=True, vmem_limit_bytes=32 * 2**20
        ),
    )(total)
    return middle.reshape(shape)


def pair_middle(total, axis, precision):
    odd = lax.axis_index(axis) % 2 == 1
    result = []
    for i in range(total.shape[0]):
        own = total[i]
        other = lax.ppermute(own, axis, [(0, 1), (1, 0), (2, 3), (3, 2)])
        pair = product(jnp.where(odd, own, other), jnp.where(odd, other, own), precision)
        far = lax.ppermute(pair, axis, [(0, 2), (2, 0), (1, 3), (3, 1)])
        result.append(product(jnp.where(odd, other, far), jnp.where(odd, far, other), precision))
    return jnp.stack(result)


def gathered_middle(total, axis, precision):
    devices = lax.axis_size(axis)
    me = lax.axis_index(axis)
    gathered = lax.all_gather(total, axis)
    middle = lax.dynamic_index_in_dim(gathered, (me + devices - 1) % devices, 0, False)
    for k in range(2, devices):
        other = lax.dynamic_index_in_dim(gathered, (me + devices - k) % devices, 0, False)
        middle = product(middle, other, precision)
    return middle


def around(parts, middle_of, precision):
    n = len(parts)
    above = [None, parts[0]]
    below = [None, parts[n - 1]]
    for r in range(1, n):
        above.append(product(parts[r], above[-1], precision))
    for r in range(n - 2, 0, -1):
        below.append(product(below[-1], parts[r], precision))
    below = below[::-1]
    middle = middle_of(above[n])
    result = []
    for r in range(n):
        value = middle
        if r:
            value = product(above[r], value, precision)
        if r < n - 1:
            value = product(value, below[r], precision)
        result.append(value)
    return result


def on_device(transfer, trunc_ranks):
    rows, cols, sectors, width, _ = transfer.shape
    exact, fine = lax.Precision.HIGHEST, lax.Precision.HIGH
    parts = [transfer[r] for r in range(rows)]
    envs = jnp.stack(around(parts, lambda t: chain_middle(t, "sec"), exact))
    blocks = orthonormal(envs.reshape(-1, width, width), trunc_ranks.reshape(-1))
    blocks = blocks.reshape(transfer.shape)
    owned = lax.all_to_all(blocks, "sect", split_axis=2, concat_axis=1, tiled=True)
    columns = [owned[:, c] for c in range(owned.shape[1])]
    middle_of = pair_middle if lax.axis_size("col") == 4 else gathered_middle
    result = around(columns, lambda t: middle_of(t, "col", fine), fine)
    return math.sqrt(width) * jnp.stack(result, axis=1)


def solution(mesh):
    in_specs = (P("sec", ("col", "sect"), None, None, None), P("sec", ("col", "sect"), None))
    out_specs = P("sec", "col", "sect", None, None)
    return jax.shard_map(
        on_device, mesh=mesh, in_specs=in_specs, out_specs=out_specs, check_vma=False
    )
```

```python
import functools
import math

import jax
import jax.numpy as jnp
from jax import lax
from jax.experimental import pallas as pl
from jax.experimental.pallas import tpu as pltpu
from jax.sharding import PartitionSpec as P

PANEL = 32
PACK = 128 // PANEL
LAG = 3
TOGETHER = 8


def product(former, latter, precision=lax.Precision.HIGHEST):
    return jnp.einsum("...ik,...kj->...ij", former, latter, precision=precision)


def split3(value):
    first = value.astype(jnp.bfloat16)
    rest = value - first.astype(jnp.float32)
    second = rest.astype(jnp.bfloat16)
    third = (rest - second.astype(jnp.float32)).astype(jnp.bfloat16)
    return first, second, third


def stack_left(value, axis):
    a, b, c = split3(value)
    return jnp.concatenate([a, a, b, a, b, c], axis=axis)


def stack_right(value, axis):
    a, b, c = split3(value)
    return jnp.concatenate([a, b, a, c, b, a], axis=axis)


def panel_inverse(groups):
    lane = lax.broadcasted_iota(jnp.int32, (8, 128), 1)
    sub = lax.broadcasted_iota(jnp.int32, (8, 128), 0)
    local = lane % PANEL
    base = lane - local
    tiles = PANEL // 8
    work = [[g[8 * r : 8 * r + 8] for r in range(tiles)] for g in groups]
    inv = [
        [jnp.where(local == sub + 8 * r, 1.0, 0.0).astype(jnp.float32) for r in range(tiles)]
        for _ in groups
    ]
    for k in range(PANEL):
        own, at = divmod(k, 8)
        index = base + k
        for a, w in zip(work, inv):
            cols = [
                jnp.take_along_axis(a[r], index, axis=1, mode="promise_in_bounds")
                for r in range(own, tiles)
            ]
            pivot = cols[0][at : at + 1]
            recip = 1.0 / pivot
            row_a = a[own][at : at + 1] * recip
            row_w = w[own][at : at + 1] * recip
            scale = lax.rsqrt(pivot)
            for r in range(own, tiles):
                m = cols[r - own]
                if r == own:
                    m = jnp.where(sub > at, m, 0.0)
                a[r] = a[r] - m * row_a
                w[r] = w[r] - m * row_w
            w[own] = w[own] * jnp.where(sub == at, scale, 1.0)
    return [jnp.concatenate(w, axis=0) for w in inv]


def orthonormal_kernel(rank_ref, env_ref, out_ref, gram_ref, inv_ref):
    count, width, _ = env_ref.shape

    def start(step, carry):
        row = lax.broadcasted_iota(jnp.int32, (width, width), 0)
        col = lax.broadcasted_iota(jnp.int32, (width, width), 1)
        some = [step * 2 + i for i in range(2)]
        values = []
        for m in some:
            rank = rank_ref[m]
            unit = jnp.where(jnp.logical_and(row == col, row >= rank), 1.0, 0.0)
            values.append(jnp.where(jnp.maximum(row, col) < rank, env_ref[m], unit))
        grams = [
            lax.dot_general(
                value,
                value,
                (((1,), (1,)), ((), ())),
                precision=lax.Precision.HIGHEST,
                preferred_element_type=jnp.float32,
            )
            for value in values
        ]
        for m, value, gram in zip(some, values, grams):
            out_ref[m] = value
            gram_ref[m] = gram
        return carry

    lax.fori_loop(0, count // 2, start, 0)

    for p in range(width // PANEL):
        lo, hi = p * PANEL, (p + 1) * PANEL
        edge = lo // 128 * 128
        groups = [
            jnp.concatenate(
                [gram_ref[g * PACK + i, lo:hi, edge : edge + 128][:, lo - edge : hi - edge] for i in range(PACK)],
                axis=1,
            )
            for g in range(count // PACK)
        ]
        for g, packed in enumerate(panel_inverse(groups)):
            for i in range(PACK):
                inv_ref[g * PACK + i] = packed[:, i * PANEL : (i + 1) * PANEL]

        def update(step, carry):
            some = [step * TOGETHER + i for i in range(TOGETHER)]
            factors = [stack_left(inv_ref[m], 1) for m in some]
            rows_g = [stack_right(gram_ref[m, lo:hi, edge:], 0) for m in some]
            rows_r = [stack_right(out_ref[m, lo:hi, :], 0) for m in some]
            done = [
                jnp.dot(f, r, preferred_element_type=jnp.float32)
                for f, r in zip(factors, rows_r)
            ]
            if hi < width:
                skip = hi % 128
                first = hi - skip
                contract = (((0,), (0,)), ((), ()))
                upper = [
                    jnp.dot(f, g, preferred_element_type=jnp.float32)[:, first - edge :]
                    for f, g in zip(factors, rows_g)
                ]
                low = [stack_left(u, 0) for u in upper]
                old_r = [out_ref[m, hi:, :] for m in some]
                old_g = [gram_ref[m, hi:, first:] for m in some]
                tail_r = [
                    lax.dot_general(
                        l, stack_right(d, 0), contract, preferred_element_type=jnp.float32
                    )[skip:]
                    for l, d in zip(low, done)
                ]
                tail_g = [
                    lax.dot_general(
                        l, stack_right(u, 0), contract, preferred_element_type=jnp.float32
                    )[skip:]
                    for l, u in zip(low, upper)
                ]
                for m, old, tail in zip(some, old_r, tail_r):
                    out_ref[m, hi:, :] = old - tail
                for m, old, tail in zip(some, old_g, tail_g):
                    gram_ref[m, hi:, first:] = old - tail
            for m, d in zip(some, done):
                out_ref[m, lo:hi, :] = d
            return carry

        lax.fori_loop(0, count // TOGETHER, update, 0)


def orthonormal(envs, ranks):
    count, width, _ = envs.shape
    vmem = pl.BlockSpec(memory_space=pltpu.VMEM)
    return pl.pallas_call(
        orthonormal_kernel,
        out_shape=jax.ShapeDtypeStruct(envs.shape, jnp.float32),
        in_specs=[pl.BlockSpec(memory_space=pltpu.SMEM), vmem],
        out_specs=vmem,
        scratch_shapes=[
            pltpu.VMEM((count, width, width), jnp.float32),
            pltpu.VMEM((count, PANEL, PANEL), jnp.float32),
        ],
        compiler_params=pltpu.CompilerParams(vmem_limit_bytes=40 * 2**20),
    )(ranks, envs)


def chain_kernel(axis, n, tot_ref, out_ref, up, down, up_out, down_out, send_u, recv_u, send_d, recv_d):
    count, width, _ = tot_ref.shape
    half = width // 2
    me = lax.axis_index(axis)
    has_prev, has_next = me > 0, me < n - 1
    inner = jnp.logical_and(has_prev, has_next)

    def up_copy(q):
        return pltpu.make_async_remote_copy(
            src_ref=up_out.at[q],
            dst_ref=up.at[q],
            send_sem=send_u.at[q],
            recv_sem=recv_u.at[q],
            device_id={axis: jnp.minimum(me + 1, n - 1)},
            device_id_type=pl.DeviceIdType.MESH,
        )

    def down_copy(q):
        return pltpu.make_async_remote_copy(
            src_ref=down_out.at[q],
            dst_ref=down.at[q],
            send_sem=send_d.at[q],
            recv_sem=recv_d.at[q],
            device_id={axis: jnp.maximum(me - 1, 0)},
            device_id_type=pl.DeviceIdType.MESH,
        )

    def dot(a, b):
        return jnp.dot(
            a, b, precision=lax.Precision.HIGHEST, preferred_element_type=jnp.float32
        )

    barrier = pltpu.get_barrier_semaphore()

    @pl.when(has_prev)
    def _():
        pl.semaphore_signal(
            barrier, inc=1, device_id={axis: me - 1}, device_id_type=pl.DeviceIdType.MESH
        )

    @pl.when(has_next)
    def _():
        pl.semaphore_signal(
            barrier, inc=1, device_id={axis: me + 1}, device_id_type=pl.DeviceIdType.MESH
        )

    @pl.when(inner)
    def _():
        pl.semaphore_wait(barrier, 2)

    @pl.when(jnp.logical_not(inner))
    def _():
        pl.semaphore_wait(barrier, 1)

    @pl.when(me == 0)
    def _():
        def send(c, carry):
            for h in range(2):
                up_out[2 * c + h] = tot_ref[c, :, h * half : (h + 1) * half]
                up_copy(2 * c + h).start()
            return carry

        lax.fori_loop(0, count, send, 0)

    @pl.when(me == n - 1)
    def _():
        def send(c, carry):
            for h in range(2):
                down_out[2 * c + h] = tot_ref[c, h * half : (h + 1) * half, :]
                down_copy(2 * c + h).start()
            return carry

        lax.fori_loop(0, count, send, 0)

    chunks = 2 * count
    far = me >= n // 2
    up_lag = jnp.where(far, LAG, 0)
    down_lag = jnp.where(far, 0, LAG)

    def one(step, carry):
        qu = step - up_lag
        qd = step - down_lag
        up_now = jnp.logical_and(qu >= 0, qu < chunks)
        down_now = jnp.logical_and(qd >= 0, qd < chunks)

        @pl.when(jnp.logical_and(has_prev, up_now))
        def _():
            up_copy(qu).wait_recv()

        @pl.when(jnp.logical_and(inner, up_now))
        def _():
            up_out[qu] = dot(tot_ref[qu // 2], up[qu])
            up_copy(qu).start()

        @pl.when(jnp.logical_and(has_next, down_now))
        def _():
            down_copy(qd).wait_recv()

        @pl.when(jnp.logical_and(inner, down_now))
        def _():
            down_out[qd] = dot(down[qd], tot_ref[qd // 2])
            down_copy(qd).start()

        both = jnp.logical_and(step > LAG, (step - LAG) % 2 == 1)
        c = (step - LAG) // 2

        @pl.when(jnp.logical_and(inner, both))
        def _():
            out_ref[c] = dot(up[2 * c], down[2 * c]) + dot(up[2 * c + 1], down[2 * c + 1])

        @pl.when(jnp.logical_and(me == 0, both))
        def _():
            for h in range(2):
                out_ref[c, h * half : (h + 1) * half, :] = down[2 * c + h]

        @pl.when(jnp.logical_and(me == n - 1, both))
        def _():
            for h in range(2):
                out_ref[c, :, h * half : (h + 1) * half] = up[2 * c + h]

        return carry

    lax.fori_loop(0, chunks + LAG, one, 0)

    def drain(q, carry):
        @pl.when(has_next)
        def _():
            up_copy(q).wait_send()

        @pl.when(has_prev)
        def _():
            down_copy(q).wait_send()

        return carry

    lax.fori_loop(0, 2 * count, drain, 0)


def chain_middle(total, axis):
    shape = total.shape
    width = shape[-1]
    total = total.reshape(-1, width, width)
    count = total.shape[0]
    vmem = pl.BlockSpec(memory_space=pltpu.VMEM)
    tall = pltpu.VMEM((2 * count, width, width // 2), jnp.float32)
    wide = pltpu.VMEM((2 * count, width // 2, width), jnp.float32)
    middle = pl.pallas_call(
        functools.partial(chain_kernel, axis, lax.axis_size(axis)),
        out_shape=jax.ShapeDtypeStruct(total.shape, jnp.float32),
        in_specs=[vmem],
        out_specs=vmem,
        scratch_shapes=[tall, wide, tall, wide] + [pltpu.SemaphoreType.DMA((2 * count,))] * 4,
        compiler_params=pltpu.CompilerParams(
            collective_id=0, has_side_effects=True, vmem_limit_bytes=32 * 2**20
        ),
    )(total)
    return middle.reshape(shape)


def pair_middle(total, axis, precision):
    odd = lax.axis_index(axis) % 2 == 1
    result = []
    for i in range(total.shape[0]):
        own = total[i]
        other = lax.ppermute(own, axis, [(0, 1), (1, 0), (2, 3), (3, 2)])
        pair = product(jnp.where(odd, own, other), jnp.where(odd, other, own), precision)
        far = lax.ppermute(pair, axis, [(0, 2), (2, 0), (1, 3), (3, 1)])
        result.append(product(jnp.where(odd, other, far), jnp.where(odd, far, other), precision))
    return jnp.stack(result)


def gathered_middle(total, axis, precision):
    devices = lax.axis_size(axis)
    me = lax.axis_index(axis)
    gathered = lax.all_gather(total, axis)
    middle = lax.dynamic_index_in_dim(gathered, (me + devices - 1) % devices, 0, False)
    for k in range(2, devices):
        other = lax.dynamic_index_in_dim(gathered, (me + devices - k) % devices, 0, False)
        middle = product(middle, other, precision)
    return middle


def around(parts, middle_of, precision):
    n = len(parts)
    above = [None, parts[0]]
    below = [None, parts[n - 1]]
    for r in range(1, n):
        above.append(product(parts[r], above[-1], precision))
    for r in range(n - 2, 0, -1):
        below.append(product(below[-1], parts[r], precision))
    below = below[::-1]
    middle = middle_of(above[n])
    result = []
    for r in range(n):
        value = middle
        if r:
            value = product(above[r], value, precision)
        if r < n - 1:
            value = product(value, below[r], precision)
        result.append(value)
    return result


def on_device(transfer, trunc_ranks):
    rows, cols, sectors, width, _ = transfer.shape
    exact, fine = lax.Precision.HIGHEST, lax.Precision.HIGH
    parts = [transfer[r] for r in range(rows)]
    envs = jnp.stack(around(parts, lambda t: chain_middle(t, "sec"), exact))
    blocks = orthonormal(envs.reshape(-1, width, width), trunc_ranks.reshape(-1))
    blocks = blocks.reshape(transfer.shape)
    owned = lax.all_to_all(blocks, "sect", split_axis=2, concat_axis=1, tiled=True)
    columns = [owned[:, c] for c in range(owned.shape[1])]
    middle_of = pair_middle if lax.axis_size("col") == 4 else gathered_middle
    result = around(columns, lambda t: middle_of(t, "col", fine), fine)
    return math.sqrt(width) * jnp.stack(result, axis=1)


def solution(mesh):
    in_specs = (P("sec", ("col", "sect"), None, None, None), P("sec", ("col", "sect"), None))
    out_specs = P("sec", "col", "sect", None, None)
    return jax.shard_map(
        on_device, mesh=mesh, in_specs=in_specs, out_specs=out_specs, check_vma=False
    )
```
